32 devices in a mesh: grp: 2 (over x), tile: 16 (over z, y, core).
Axes of the slice: x: 2, y: 2, z: 4, core: 2. Of those that a mesh axis runs over, the one named last changes fastest.
Arguments:
- acts: bfloat16 [256, 4096], P(('grp', 'tile')), parts along dimension 0, may hold values from -6 to 6
- grads: bfloat16 [256, 4096], P(('grp', 'tile')), parts along dimension 0, may hold values from -6 to 6
- basis_in: bfloat16 [4096, 4096], P('tile'), may hold values from -0.09375 to 0.09375
- basis_out: bfloat16 [4096, 4096], P('tile'), may hold values from -0.09375 to 0.09375
Outputs:
- corr_tiles: float32 [32, 512, 2048], P(('grp', 'tile')), parts along dimension 0
The draws below stay inside these ranges and needn't reach their ends.
There are 2 independent parts, one for each index of `grp`. The reference program is written for one: setup_inputs(seed, part) draws one part's arguments, and reference() takes and returns one part's arrays. A program takes and returns all parts, laid end to end along the dimension named above; an argument that names none is the same for every part. Nothing has to cross between parts.
All inputs are finite; a program needn't handle non-finite values.
Results may differ from the reference program's by a relative error of at most 0.005.
Values may be sent and summed in bfloat16 or wider, within the bound.
A program may use at most 128 MiB of HBM per device.

```python
import jax
import jax.numpy as jnp
from jax import lax

D_IN = 4096
D_OUT = 4096
SEQ = 128
ROWB = 8
TOKENS = 128
EXAMPLES = 1
COLB = 2
TILE_R = 512
TILE_C = 2048
N_TILE = 16


def block_scale(stream_key, dims, split, least, largest):
    factor_of, own = 1.0, jax.random.fold_in(stream_key, 6)
    for axis_at, shards_of in split:
        draws = jnp.exp(jax.random.uniform(jax.random.fold_in(own, axis_at), (shards_of,), jnp.float32, least / len(split), largest / len(split)))
        factor_of = factor_of * jnp.repeat(draws, dims[axis_at] // shards_of).reshape([-1 if axis == axis_at else 1 for axis in range(len(dims))])
    return factor_of


def gaussian(rng, shape, scale, limit, cuts=(), kind=jnp.bfloat16):
    gain = block_scale(rng, shape, cuts, -0.22, 0.18) if cuts else 1.0
    array = jax.random.normal(rng, shape, jnp.float32) * scale * gain
    return jnp.minimum(jnp.maximum(array, -limit), limit).astype(kind)


def setup_inputs(seed: int = 0, part: int = 0) -> dict:
    key_of = jax.random.split(jax.random.key(seed), 5)
    part_splits = jax.random.split(jax.random.fold_in(key_of[4], part), 5)
    return {
        "acts": gaussian(part_splits[0], (TOKENS, D_IN), 1.0, 6.0, ((0, 16),)),
        "grads": gaussian(part_splits[1], (TOKENS, D_OUT), 1.0, 6.0, ((0, 16),)),
        "basis_in": gaussian(key_of[2], (D_IN, D_IN), D_IN ** -0.5, 0.09375, ((0, 16),)),
        "basis_out": gaussian(key_of[3], (D_OUT, D_OUT), D_OUT ** -0.5, 0.09375, ((0, 16),)),
    }


def rotate(values, basis):
    product = jnp.dot(values.astype(jnp.float32), basis.astype(jnp.float32), precision=lax.Precision.HIGHEST)
    return product.astype(jnp.bfloat16)


def reference(acts, grads, basis_in, basis_out):
    acts_rot = rotate(acts, basis_in)
    grads_rot = rotate(grads, basis_out)
    acts_ex = acts_rot.reshape(EXAMPLES, SEQ, D_IN)
    grads_ex = grads_rot.reshape(EXAMPLES, SEQ, D_OUT)

    def accumulate(total, pair):
        grad_part, act_part = pair
        rotated = jnp.dot(grad_part.astype(jnp.float32).T, act_part.astype(jnp.float32), precision=lax.Precision.HIGHEST)
        return total + rotated * rotated, None

    start = jnp.zeros((D_OUT, D_IN), jnp.float32)
    total, _ = lax.scan(accumulate, start, (grads_ex, acts_ex))
    corr = total / float(EXAMPLES * SEQ)
    tiled = corr.reshape(ROWB, TILE_R, COLB, TILE_C).transpose(0, 2, 1, 3)
    return tiled.reshape(N_TILE, TILE_R, TILE_C)
```

```python
import functools

import jax
import jax.numpy as jnp
from jax import lax
from jax.experimental import pallas as pl
from jax.experimental.pallas import tpu as pltpu
from jax.sharding import PartitionSpec as P

SEQ = 128
ROWB = 8
CORES = 2
YS = 2
MESH = pl.DeviceIdType.MESH
F32 = jnp.float32
BF16 = jnp.bfloat16


def rotate_kernel(
    zs,
    acts_ref, grads_ref, bin_hbm, bout_hbm,
    aout_ref, gout_ref,
    x, r, bi, bo,
    ca_own, ca_send, ca_recv, cg_own, cg_send, cg_recv,
    ya_send, ya_recv, yg_send, yg_recv,
    za_send, za_recv, zg_send, zg_recv,
    ag, gx,
    basis_sem, tok_s, tok_r,
    ca_s, ca_r, cg_s, cg_r,
    ya_s, ya_r, yg_s, yg_r,
    za_s, za_r, zg_s, zg_r,
    agz_s, agz_r, agy_s, agy_r, gx_s, gx_r,
):
    n = CORES * YS * zs
    tok = acts_ref.shape[0]
    depth = bi.shape[0]
    half_rows = gx.shape[1]
    gcols = gx.shape[2]
    acols = ag.shape[-1]
    me = lax.axis_index("tile")
    c = lax.rem(me, CORES)
    y = lax.rem(me // CORES, YS)
    z = me // (CORES * YS)
    sib = me + 1 - 2 * c
    yp = me + CORES * (1 - 2 * y)
    oc, oy = 1 - c, 1 - y

    def remote(src, dst, ssem, rsem, dev):
        return pltpu.make_async_remote_copy(
            src_ref=src, dst_ref=dst, send_sem=ssem, recv_sem=rsem,
            device_id={"tile": dev}, device_id_type=MESH,
        )

    load_in = pltpu.make_async_copy(bin_hbm, bi, basis_sem.at[0])
    load_out = pltpu.make_async_copy(bout_hbm, bo, basis_sem.at[1])
    load_out.start()
    load_in.start()

    barrier = pltpu.get_barrier_semaphore()

    def greet(i, carry):
        pl.semaphore_signal(
            barrier, inc=1, device_id={"tile": lax.rem(me + i, n)}, device_id_type=MESH
        )
        return carry

    lax.fori_loop(1, n, greet, 0)
    x[...] = jnp.concatenate(
        [acts_ref[...].astype(F32), grads_ref[...].astype(F32)], axis=0
    ).astype(BF16)
    pl.semaphore_wait(barrier, n - 1)

    def tok_copy(to, frm):
        return remote(
            x.at[:, pl.ds(pl.multiple_of(to * depth, depth), depth)],
            r.at[frm], tok_s.at[to], tok_r.at[frm], to,
        )

    def send_tok(i, carry):
        tok_copy(lax.rem(me + i, n), me).start()
        return carry

    lax.fori_loop(1, n, send_tok, 0)
    r[pl.ds(me, 1)] = x[:, pl.ds(pl.multiple_of(me * depth, depth), depth)][None]

    def recv_tok(i, carry):
        tok_copy(me, lax.rem(me + n - i, n)).wait_recv()
        return carry

    lax.fori_loop(1, n, recv_tok, 0)
    both = r[...].astype(F32)
    a = both[:, :tok].reshape(n * tok, depth).astype(BF16)
    g = both[:, tok:].reshape(n * tok, depth).astype(BF16)
    load_out.wait()
    load_in.wait()


    def core_a(yy, zz):
        return remote(
            ca_send.at[yy, zz], ca_recv.at[yy, zz], ca_s.at[yy, zz], ca_r.at[yy, zz], sib
        )

    def core_g(yy, zz):
        return remote(
            cg_send.at[yy, zz], cg_recv.at[yy, zz], cg_s.at[yy, zz], cg_r.at[yy, zz], sib
        )

    def acol(cc, yy, zz):
        start = ((cc * YS + yy) * zs + zz) * acols
        return pl.ds(pl.multiple_of(start, acols), acols)

    def make_chunk(yy, zz):
        ca_send[yy, zz] = jnp.dot(a, bi[:, acol(oc, yy, zz)], preferred_element_type=F32)
        core_a(yy, zz).start()
        gpart = jnp.dot(
            g,
            bo[:, pl.ds(pl.multiple_of((zz * YS + yy) * gcols, gcols), gcols)],
            preferred_element_type=F32,
        )
        low, high = gpart[:half_rows], gpart[half_rows:]
        cg_send[yy, zz] = jnp.where(c == 0, high, low)
        core_g(yy, zz).start()
        cg_own[yy, zz] = jnp.where(c == 0, low, high)
        ca_own[yy, zz] = jnp.dot(a, bi[:, acol(c, yy, zz)], preferred_element_type=F32)

    def y_a(zz):
        return remote(ya_send.at[zz], ya_recv.at[zz], ya_s.at[zz], ya_r.at[zz], yp)

    def y_g(zz):
        return remote(yg_send.at[zz], yg_recv.at[zz], yg_s.at[zz], yg_r.at[zz], yp)

    def zdev(zz):
        return zz * (CORES * YS) + lax.rem(me, CORES * YS)

    def z_a(to, frm):
        return remote(za_send.at[to], za_recv.at[frm], za_s.at[to], za_r.at[frm], zdev(to))

    def z_g(to, frm):
        return remote(zg_send.at[to], zg_recv.at[frm], zg_s.at[to], zg_r.at[frm], zdev(to))

    order = [lax.rem(z + 1 + i, zs) for i in range(zs)]

    for zz in order:
        make_chunk(oy, zz)
    for zz in order:
        core_a(oy, zz).wait_recv()
        ya_send[zz] = (ca_own[oy, zz] + ca_recv[oy, zz]).astype(BF16)
        y_a(zz).start()
        core_g(oy, zz).wait_recv()
        yg_send[zz] = (cg_own[oy, zz] + cg_recv[oy, zz]).astype(BF16)
        y_g(zz).start()
        make_chunk(y, zz)
    for i, zz in enumerate(order):
        core_a(y, zz).wait_recv()
        y_a(zz).wait_recv()
        total = ca_own[y, zz] + ca_recv[y, zz] + ya_recv[zz].astype(F32)
        if i < zs - 1:
            za_send[zz] = total.astype(BF16)
            z_a(zz, z).start()
        else:
            ca_own[y, zz] = total
        core_g(y, zz).wait_recv()
        y_g(zz).wait_recv()
        total = cg_own[y, zz] + cg_recv[y, zz] + yg_recv[zz].astype(F32)
        if i < zs - 1:
            zg_send[zz] = total.astype(BF16)
            z_g(zz, z).start()
        else:
            cg_own[y, zz] = total

    others = [lax.rem(z + zs - 1 - i, zs) for i in range(zs - 1)]
    total = ca_own[y, z]
    for zz in others:
        z_a(z, zz).wait_recv()
        total = total + za_recv[zz].astype(F32)
    ag[y, z] = total.astype(BF16)

    def ag_z(to, frm):
        return remote(ag.at[y, frm], ag.at[y, frm], agz_s.at[to], agz_r.at[frm], zdev(to))

    def ag_y(yy, zz):
        return remote(ag.at[yy, zz], ag.at[yy, zz], agy_s.at[zz], agy_r.at[zz], yp)

    for zz in order[:-1]:
        ag_z(zz, z).start()
    ag_y(y, z).start()

    total = cg_own[y, z]
    for zz in others:
        z_g(z, zz).wait_recv()
        total = total + zg_recv[zz].astype(F32)
    gx[c] = total
    swap = remote(gx.at[c], gx.at[c], gx_s, gx_r, sib)
    swap.start()

    for zz in others:
        ag_z(z, zz).wait_recv()
        ag_y(y, zz).start()
    aout_ref[y] = ag[y]
    remote(gx.at[oc], gx.at[oc], gx_s, gx_r, sib).wait_recv()
    gout_ref[...] = gx[...]
    for zz in [z] + others:
        ag_y(oy, zz).wait_recv()
        aout_ref[oy, zz] = ag[oy, zz]

    def sent_tok(i, carry):
        tok_copy(lax.rem(me + i, n), me).wait_send()
        return carry

    lax.fori_loop(1, n, sent_tok, 0)
    for zz in order:
        core_a(oy, zz).wait_send()
        core_g(oy, zz).wait_send()
        core_a(y, zz).wait_send()
        core_g(y, zz).wait_send()
        y_a(zz).wait_send()
        y_g(zz).wait_send()
        ag_y(y, zz).wait_send()
    for zz in order[:-1]:
        z_a(zz, z).wait_send()
        z_g(zz, z).wait_send()
        ag_z(zz, z).wait_send()
    swap.wait_send()


def rotate(acts, grads, basis_in, basis_out, tiles):
    zs = tiles // (CORES * YS)
    tok, width_in = acts.shape
    width_out = grads.shape[1]
    depth = basis_in.shape[0]
    tokens = tok * tiles
    half = tokens // CORES
    acols = width_in // tiles
    gcols = width_out // ROWB
    a_grid, g_grid = (YS, zs, tokens, acols), (YS, zs, half, gcols)
    dma = pltpu.SemaphoreType.DMA
    scratch = [
        pltpu.VMEM((2 * tok, width_in), BF16),
        pltpu.VMEM((tiles, 2 * tok, depth), BF16),
        pltpu.VMEM((depth, width_in), BF16),
        pltpu.VMEM((depth, width_out), BF16),
    ]
    scratch += [pltpu.VMEM(a_grid, F32)] * 3 + [pltpu.VMEM(g_grid, F32)] * 3
    for _ in range(2):
        scratch += [pltpu.VMEM(a_grid[1:], BF16)] * 2 + [pltpu.VMEM(g_grid[1:], BF16)] * 2
    scratch += [pltpu.VMEM(a_grid, BF16), pltpu.VMEM((CORES, half, gcols), F32)]
    scratch += [dma((2,)), dma((tiles,)), dma((tiles,))]
    scratch += [dma((YS, zs))] * 4 + [dma((zs,))] * 12 + [dma, dma]
    return pl.pallas_call(
        functools.partial(rotate_kernel, zs),
        out_shape=(
            jax.ShapeDtypeStruct(a_grid, BF16),
            jax.ShapeDtypeStruct((CORES, half, gcols), F32),
        ),
        in_specs=[pl.BlockSpec(memory_space=pltpu.VMEM)] * 2
        + [pl.BlockSpec(memory_space=pl.ANY)] * 2,
        out_specs=(pl.BlockSpec(memory_space=pltpu.VMEM),) * 2,
        scratch_shapes=scratch,
        compiler_params=pltpu.CompilerParams(
            collective_id=0, has_side_effects=True, vmem_limit_bytes=40 * 1024 * 1024
        ),
        name="rotate",
    )(acts, grads, basis_in, basis_out)


def correct_kernel(scale, a_ref, g_ref, out_ref, lhs):
    tokens = g_ref.shape[0]

    @pl.when(pl.program_id(0) == 0)
    def _():
        gt = g_ref[...].T
        high = gt.astype(BF16)
        lhs[:, :tokens] = high
        lhs[:, tokens:] = (gt - high.astype(F32)).astype(BF16)

    a = a_ref[0]
    rotated = jnp.dot(
        lhs[...], jnp.concatenate([a, a], axis=0), preferred_element_type=F32
    )
    out_ref[0] = rotated * rotated * scale


def correct(a, g):
    blocks, tokens, acols = a.shape
    rows = g.shape[1]
    return pl.pallas_call(
        functools.partial(correct_kernel, 1.0 / tokens),
        grid=(blocks,),
        out_shape=jax.ShapeDtypeStruct((1, rows, blocks * acols), F32),
        in_specs=[
            pl.BlockSpec((1, tokens, acols), lambda i: (i, 0, 0)),
            pl.BlockSpec((tokens, rows), lambda i: (0, 0)),
        ],
        out_specs=pl.BlockSpec((1, rows, acols), lambda i: (0, 0, i)),
        scratch_shapes=[pltpu.VMEM((rows, 2 * tokens), BF16)],
        compiler_params=pltpu.CompilerParams(vmem_limit_bytes=16 * 1024 * 1024),
        name="correct",
    )(a, g)


def chip_body(acts, grads, basis_in, basis_out):
    tiles = lax.axis_size("tile")
    a, g = rotate(acts, grads, basis_in, basis_out, tiles)
    tokens = a.shape[2]
    return correct(a.reshape(-1, tokens, a.shape[3]), g.reshape(tokens, g.shape[2]))


def body(acts, grads, basis_in, basis_out):
    tiles = lax.axis_size("tile")
    tok_rows = acts.shape[0]
    width_in = acts.shape[1]
    width_out = grads.shape[1]
    col_blocks = tiles // ROWB
    tile_rows_n = width_out // ROWB
    tile_cols_n = width_in // col_blocks
    acts_feat, grads_feat = (
        lax.all_to_all(acts, "tile", split_axis=1, concat_axis=0, tiled=True),
        lax.all_to_all(grads, "tile", split_axis=1, concat_axis=0, tiled=True),
    )
    acts_rot = lax.psum_scatter(
        jnp.dot(acts_feat, basis_in, preferred_element_type=jnp.float32),
        "tile",
        scatter_dimension=0,
        tiled=True,
    ).astype(jnp.bfloat16)
    grads_rot = lax.psum_scatter(
        jnp.dot(grads_feat, basis_out, preferred_element_type=jnp.float32),
        "tile",
        scatter_dimension=0,
        tiled=True,
    ).astype(jnp.bfloat16)
    grad_send = jnp.repeat(grads_rot.reshape(tok_rows, ROWB, tile_rows_n), col_blocks, axis=1)
    act_send = jnp.tile(acts_rot.reshape(tok_rows, col_blocks, tile_cols_n), (1, ROWB, 1))
    grad_tile, act_tile = (
        lax.all_to_all(grad_send, "tile", split_axis=1, concat_axis=0, tiled=True),
        lax.all_to_all(act_send, "tile", split_axis=1, concat_axis=0, tiled=True),
    )
    grad_tile = grad_tile.reshape(tok_rows * tiles, tile_rows_n)
    act_tile = act_tile.reshape(tok_rows * tiles, tile_cols_n)
    total_rows = grad_tile.shape[0]
    examples = total_rows // SEQ
    grad_ex = grad_tile.reshape(examples, SEQ, tile_rows_n)
    act_ex = act_tile.reshape(examples, SEQ, tile_cols_n)

    def accumulate(index, total):
        grad_part = grad_ex[index]
        act_part = act_ex[index]
        rotated = lax.dot_general(
            grad_part, act_part, (((0,), (0,)), ((), ())), preferred_element_type=jnp.float32
        )
        return total + rotated * rotated

    start = jnp.zeros((tile_rows_n, tile_cols_n), jnp.float32)
    total = lax.fori_loop(0, examples, accumulate, start)
    corr = total / float(examples * SEQ)
    return corr[None]


def solution(mesh):
    in_specs = (
        P(("grp", "tile"), None),
        P(("grp", "tile"), None),
        P("tile", None),
        P("tile", None),
    )
    out_specs = P(("grp", "tile"), None, None)

    def whole(acts, grads, basis_in, basis_out):
        tiles = mesh.shape["tile"]
        tokens = acts.shape[0] // mesh.shape["grp"]
        per_chip = tiles == CORES * ROWB and tokens == SEQ
        return jax.shard_map(
            chip_body if per_chip else body,
            mesh=mesh, in_specs=in_specs, out_specs=out_specs, check_vma=False,
        )(acts, grads, basis_in, basis_out)

    return whole
```

```python
import functools

import jax
import jax.numpy as jnp
from jax import lax
from jax.experimental import pallas as pl
from jax.experimental.pallas import tpu as pltpu
from jax.sharding import PartitionSpec as P

SEQ = 128
ROWB = 8
CORES = 2
YS = 2
MESH = pl.DeviceIdType.MESH
VMEM_LIMIT = 62 * 1024 * 1024
F32 = jnp.float32
BF16 = jnp.bfloat16


def rotate_kernel(
    zs,
    acts_hbm, grads_hbm, bin_hbm, bout_hbm,
    aout_ref, gout_ref,
    acts_ref, grads_ref, x, r, bi, bo,
    ca_own, ca_send, ca_recv, cg_own, cg_send, cg_recv,
    ya_send, ya_recv, yg_send, yg_recv,
    za_send, za_recv, zg_send, zg_recv,
    ag, gx,
    basis_sem, tok_s, tok_r,
    ca_s, ca_r, cg_s, cg_r,
    ya_s, ya_r, yg_s, yg_r,
    za_s, za_r, zg_s, zg_r,
    agz_s, agz_r, agy_s, agy_r, gx_s, gx_r,
):
    n = CORES * YS * zs
    tok = acts_ref.shape[0]
    depth = bi.shape[0]
    half_rows = gx.shape[1]
    gcols = gx.shape[2]
    acols = ag.shape[-1]
    me = lax.axis_index("tile")
    c = lax.rem(me, CORES)
    y = lax.rem(me // CORES, YS)
    z = me // (CORES * YS)
    sib = me + 1 - 2 * c
    yp = me + CORES * (1 - 2 * y)
    oc, oy = 1 - c, 1 - y

    def remote(src, dst, ssem, rsem, dev):
        return pltpu.make_async_remote_copy(
            src_ref=src, dst_ref=dst, send_sem=ssem, recv_sem=rsem,
            device_id={"tile": dev}, device_id_type=MESH,
        )

    load_in = pltpu.make_async_copy(bin_hbm, bi, basis_sem.at[0])
    load_out = pltpu.make_async_copy(bout_hbm, bo, basis_sem.at[1])
    load_a = pltpu.make_async_copy(acts_hbm, acts_ref, basis_sem.at[2])
    load_g = pltpu.make_async_copy(grads_hbm, grads_ref, basis_sem.at[3])
    load_a.start()
    load_g.start()
    load_in.start()
    load_out.start()

    barrier = pltpu.get_barrier_semaphore()

    def greet(i, carry):
        pl.semaphore_signal(
            barrier, inc=1, device_id={"tile": lax.rem(me + i, n)}, device_id_type=MESH
        )
        return carry

    lax.fori_loop(1, n, greet, 0)
    load_a.wait()
    load_g.wait()
    x[...] = jnp.concatenate(
        [acts_ref[...].astype(F32), grads_ref[...].astype(F32)], axis=0
    ).astype(BF16)
    pl.semaphore_wait(barrier, n - 1)

    def tok_copy(to, frm):
        return remote(
            x.at[:, pl.ds(pl.multiple_of(to * depth, depth), depth)],
            r.at[frm], tok_s.at[to], tok_r.at[frm], to,
        )

    def send_tok(i, carry):
        tok_copy(lax.rem(me + i, n), me).start()
        return carry

    lax.fori_loop(1, n, send_tok, 0)
    r[pl.ds(me, 1)] = x[:, pl.ds(pl.multiple_of(me * depth, depth), depth)][None]

    def recv_tok(i, carry):
        tok_copy(me, lax.rem(me + n - i, n)).wait_recv()
        return carry

    lax.fori_loop(1, n, recv_tok, 0)
    both = r[...].astype(F32)
    a = both[:, :tok].reshape(n * tok, depth).astype(BF16)
    g = both[:, tok:].reshape(n * tok, depth).astype(BF16)
    load_out.wait()
    load_in.wait()


    def core_a(yy, zz):
        return remote(
            ca_send.at[yy, zz], ca_recv.at[yy, zz], ca_s.at[yy, zz], ca_r.at[yy, zz], sib
        )

    def core_g(yy, zz):
        return remote(
            cg_send.at[yy, zz], cg_recv.at[yy, zz], cg_s.at[yy, zz], cg_r.at[yy, zz], sib
        )

    def acol(cc, yy, zz):
        start = ((cc * YS + yy) * zs + zz) * acols
        return pl.ds(pl.multiple_of(start, acols), acols)

    def send_a(yy, zz):
        ca_send[yy, zz] = jnp.dot(a, bi[:, acol(oc, yy, zz)], preferred_element_type=F32)
        core_a(yy, zz).start()

    def keep_a(yy, zz):
        ca_own[yy, zz] = jnp.dot(a, bi[:, acol(c, yy, zz)], preferred_element_type=F32)

    def make_g(yy, zz):
        gpart = jnp.dot(
            g,
            bo[:, pl.ds(pl.multiple_of((zz * YS + yy) * gcols, gcols), gcols)],
            preferred_element_type=F32,
        )
        low, high = gpart[:half_rows], gpart[half_rows:]
        cg_send[yy, zz] = jnp.where(c == 0, high, low)
        core_g(yy, zz).start()
        cg_own[yy, zz] = jnp.where(c == 0, low, high)

    def y_a(zz):
        return remote(ya_send.at[zz], ya_recv.at[zz], ya_s.at[zz], ya_r.at[zz], yp)

    def y_g(zz):
        return remote(yg_send.at[zz], yg_recv.at[zz], yg_s.at[zz], yg_r.at[zz], yp)

    def zdev(zz):
        return zz * (CORES * YS) + lax.rem(me, CORES * YS)

    def z_a(to, frm):
        return remote(za_send.at[to], za_recv.at[frm], za_s.at[to], za_r.at[frm], zdev(to))

    def z_g(to, frm):
        return remote(zg_send.at[to], zg_recv.at[frm], zg_s.at[to], zg_r.at[frm], zdev(to))

    order = [lax.rem(z + 1 + i, zs) for i in range(zs)]

    others = [lax.rem(z + zs - 1 - i, zs) for i in range(zs - 1)]

    for zz in order:
        send_a(oy, zz)
    for zz in order:
        keep_a(oy, zz)
        core_a(oy, zz).wait_recv()
        ya_send[zz] = (ca_own[oy, zz] + ca_recv[oy, zz]).astype(BF16)
        y_a(zz).start()
    for zz in order:
        send_a(y, zz)
        keep_a(y, zz)
    for zz in order:
        make_g(oy, zz)
    for i, zz in enumerate(order):
        core_a(y, zz).wait_recv()
        y_a(zz).wait_recv()
        total = ca_own[y, zz] + ca_recv[y, zz] + ya_recv[zz].astype(F32)
        if i < zs - 1:
            za_send[zz] = total.astype(BF16)
            z_a(zz, z).start()
        else:
            ca_own[y, zz] = total
        core_g(oy, zz).wait_recv()
        yg_send[zz] = (cg_own[oy, zz] + cg_recv[oy, zz]).astype(BF16)
        y_g(zz).start()
        make_g(y, zz)

    total = ca_own[y, z]
    for zz in others:
        z_a(z, zz).wait_recv()
        total = total + za_recv[zz].astype(F32)
    ag[y, z] = total.astype(BF16)

    def ag_z(to, frm):
        return remote(ag.at[y, frm], ag.at[y, frm], agz_s.at[to], agz_r.at[frm], zdev(to))

    def ag_y(yy, zz):
        return remote(ag.at[yy, zz], ag.at[yy, zz], agy_s.at[zz], agy_r.at[zz], yp)

    for zz in order[:-1]:
        ag_z(zz, z).start()
    ag_y(y, z).start()

    def finish_g(i):
        zz = order[i]
        core_g(y, zz).wait_recv()
        y_g(zz).wait_recv()
        total = cg_own[y, zz] + cg_recv[y, zz] + yg_recv[zz].astype(F32)
        if i < zs - 1:
            zg_send[zz] = total.astype(BF16)
            z_g(zz, z).start()
        else:
            cg_own[y, zz] = total

    for i in range(zs - 1):
        finish_g(i)
    for zz in others:
        ag_z(z, zz).wait_recv()
        ag_y(y, zz).start()
    finish_g(zs - 1)

    total = cg_own[y, z]
    for zz in others:
        z_g(z, zz).wait_recv()
        total = total + zg_recv[zz].astype(F32)
    gx[c] = total
    swap = remote(gx.at[c], gx.at[c], gx_s, gx_r, sib)
    swap.start()
    aout_ref[y] = ag[y]
    remote(gx.at[oc], gx.at[oc], gx_s, gx_r, sib).wait_recv()
    gt = gx[...].reshape(CORES * half_rows, gcols).T
    high = gt.astype(BF16)
    gout_ref[:, : CORES * half_rows] = high
    gout_ref[:, CORES * half_rows :] = (gt - high.astype(F32)).astype(BF16)
    for zz in [z] + others:
        ag_y(oy, zz).wait_recv()
        aout_ref[oy, zz] = ag[oy, zz]

    def sent_tok(i, carry):
        tok_copy(lax.rem(me + i, n), me).wait_send()
        return carry

    lax.fori_loop(1, n, sent_tok, 0)
    for zz in order:
        core_a(oy, zz).wait_send()
        core_g(oy, zz).wait_send()
        core_a(y, zz).wait_send()
        core_g(y, zz).wait_send()
        y_a(zz).wait_send()
        y_g(zz).wait_send()
        ag_y(y, zz).wait_send()
    for zz in order[:-1]:
        z_a(zz, z).wait_send()
        z_g(zz, z).wait_send()
        ag_z(zz, z).wait_send()
    swap.wait_send()


def rotate(acts, grads, basis_in, basis_out, tiles):
    zs = tiles // (CORES * YS)
    tok, width_in = acts.shape
    width_out = grads.shape[1]
    depth = basis_in.shape[0]
    tokens = tok * tiles
    half = tokens // CORES
    acols = width_in // tiles
    gcols = width_out // ROWB
    a_grid, g_grid = (YS, zs, tokens, acols), (YS, zs, half, gcols)
    dma = pltpu.SemaphoreType.DMA
    scratch = [pltpu.VMEM(acts.shape, BF16), pltpu.VMEM(grads.shape, BF16)]
    scratch += [
        pltpu.VMEM((2 * tok, width_in), BF16),
        pltpu.VMEM((tiles, 2 * tok, depth), BF16),
        pltpu.VMEM((depth, width_in), BF16),
        pltpu.VMEM((depth, width_out), BF16),
    ]
    scratch += [pltpu.VMEM(a_grid, F32)] * 3 + [pltpu.VMEM(g_grid, F32)] * 3
    for _ in range(2):
        scratch += [pltpu.VMEM(a_grid[1:], BF16)] * 2 + [pltpu.VMEM(g_grid[1:], BF16)] * 2
    scratch += [pltpu.VMEM(a_grid, BF16), pltpu.VMEM((CORES, half, gcols), F32)]
    scratch += [dma((4,)), dma((tiles,)), dma((tiles,))]
    scratch += [dma((YS, zs))] * 4 + [dma((zs,))] * 12 + [dma, dma]
    return pl.pallas_call(
        functools.partial(rotate_kernel, zs),
        out_shape=(
            jax.ShapeDtypeStruct(a_grid, BF16),
            jax.ShapeDtypeStruct((gcols, 2 * tokens), BF16),
        ),
        in_specs=[pl.BlockSpec(memory_space=pl.ANY)] * 4,
        out_specs=(pl.BlockSpec(memory_space=pltpu.VMEM),) * 2,
        scratch_shapes=scratch,
        compiler_params=pltpu.CompilerParams(
            collective_id=0, has_side_effects=True, vmem_limit_bytes=VMEM_LIMIT
        ),
        name="rotate",
    )(acts, grads, basis_in, basis_out)


def correct_kernel(scale, a_ref, g_ref, out_ref):
    acols = a_ref.shape[2]
    for k in range(a_ref.shape[0]):
        a = a_ref[k]
        rotated = jnp.dot(
            g_ref[...], jnp.concatenate([a, a], axis=0), preferred_element_type=F32
        )
        out_ref[0, :, k * acols : (k + 1) * acols] = rotated * rotated * scale


def correct(a, g):
    blocks, tokens, acols = a.shape
    rows = g.shape[0]
    step = 2
    return pl.pallas_call(
        functools.partial(correct_kernel, 1.0 / tokens),
        grid=(blocks // step,),
        out_shape=jax.ShapeDtypeStruct((1, rows, blocks * acols), F32),
        in_specs=[
            pl.BlockSpec((step, tokens, acols), lambda i: (i, 0, 0)),
            pl.BlockSpec((rows, 2 * tokens), lambda i: (0, 0)),
        ],
        out_specs=pl.BlockSpec((1, rows, step * acols), lambda i: (0, 0, i)),
        compiler_params=pltpu.CompilerParams(vmem_limit_bytes=VMEM_LIMIT),
        name="correct",
    )(a, g)


def chip_body(acts, grads, basis_in, basis_out):
    tiles = lax.axis_size("tile")
    a, g = rotate(acts, grads, basis_in, basis_out, tiles)
    tokens = a.shape[2]
    return correct(a.reshape(-1, tokens, a.shape[3]), g)


def body(acts, grads, basis_in, basis_out):
    tiles = lax.axis_size("tile")
    tok_rows = acts.shape[0]
    width_in = acts.shape[1]
    width_out = grads.shape[1]
    col_blocks = tiles // ROWB
    tile_rows_n = width_out // ROWB
    tile_cols_n = width_in // col_blocks
    acts_feat, grads_feat = (
        lax.all_to_all(acts, "tile", split_axis=1, concat_axis=0, tiled=True),
        lax.all_to_all(grads, "tile", split_axis=1, concat_axis=0, tiled=True),
    )
    acts_rot = lax.psum_scatter(
        jnp.dot(acts_feat, basis_in, preferred_element_type=jnp.float32),
        "tile",
        scatter_dimension=0,
        tiled=True,
    ).astype(jnp.bfloat16)
    grads_rot = lax.psum_scatter(
        jnp.dot(grads_feat, basis_out, preferred_element_type=jnp.float32),
        "tile",
        scatter_dimension=0,
        tiled=True,
    ).astype(jnp.bfloat16)
    grad_send = jnp.repeat(grads_rot.reshape(tok_rows, ROWB, tile_rows_n), col_blocks, axis=1)
    act_send = jnp.tile(acts_rot.reshape(tok_rows, col_blocks, tile_cols_n), (1, ROWB, 1))
    grad_tile, act_tile = (
        lax.all_to_all(grad_send, "tile", split_axis=1, concat_axis=0, tiled=True),
        lax.all_to_all(act_send, "tile", split_axis=1, concat_axis=0, tiled=True),
    )
    grad_tile = grad_tile.reshape(tok_rows * tiles, tile_rows_n)
    act_tile = act_tile.reshape(tok_rows * tiles, tile_cols_n)
    total_rows = grad_tile.shape[0]
    examples = total_rows // SEQ
    grad_ex = grad_tile.reshape(examples, SEQ, tile_rows_n)
    act_ex = act_tile.reshape(examples, SEQ, tile_cols_n)

    def accumulate(index, total):
        grad_part = grad_ex[index]
        act_part = act_ex[index]
        rotated = lax.dot_general(
            grad_part, act_part, (((0,), (0,)), ((), ())), preferred_element_type=jnp.float32
        )
        return total + rotated * rotated

    start = jnp.zeros((tile_rows_n, tile_cols_n), jnp.float32)
    total = lax.fori_loop(0, examples, accumulate, start)
    corr = total / float(examples * SEQ)
    return corr[None]


def solution(mesh):
    in_specs = (
        P(("grp", "tile"), None),
        P(("grp", "tile"), None),
        P("tile", None),
        P("tile", None),
    )
    out_specs = P(("grp", "tile"), None, None)

    def whole(acts, grads, basis_in, basis_out):
        tiles = mesh.shape["tile"]
        tokens = acts.shape[0] // mesh.shape["grp"]
        per_chip = tiles == CORES * ROWB and tokens == SEQ
        return jax.shard_map(
            chip_body if per_chip else body,
            mesh=mesh, in_specs=in_specs, out_specs=out_specs, check_vma=False,
        )(acts, grads, basis_in, basis_out)

    return whole
```

```python
import functools

import jax
import jax.numpy as jnp
from jax import lax
from jax.experimental import pallas as pl
from jax.experimental.pallas import tpu as pltpu
from jax.sharding import PartitionSpec as P

SEQ = 128
ROWB = 8
CORES = 2
YS = 2
MESH = pl.DeviceIdType.MESH
VMEM_LIMIT = 52 * 1024 * 1024
F32 = jnp.float32
BF16 = jnp.bfloat16


def rotate_kernel(
    zs,
    x, bin_hbm, bout_hbm,
    aout_ref, gout_ref,
    r, bi, bo,
    ca_own, ca_send, ca_recv, cg_own, cg_send, cg_recv,
    ya_send, ya_recv, yg_send, yg_recv,
    za_send, za_recv, zg_send, zg_recv,
    ag, gx,
    basis_sem, tok_s, tok_r,
    ca_s, ca_r, cg_s, cg_r,
    ya_s, ya_r, yg_s, yg_r,
    za_s, za_r, zg_s, zg_r,
    agz_s, agz_r, agy_s, agy_r, gx_s, gx_r,
):
    n = CORES * YS * zs
    tok = x.shape[0] // 2
    depth = bi.shape[0]
    half_rows = gx.shape[1]
    gcols = gx.shape[2]
    acols = ag.shape[-1]
    me = lax.axis_index("tile")
    c = lax.rem(me, CORES)
    y = lax.rem(me // CORES, YS)
    z = me // (CORES * YS)
    sib = me + 1 - 2 * c
    yp = me + CORES * (1 - 2 * y)
    oc, oy = 1 - c, 1 - y

    def remote(src, dst, ssem, rsem, dev):
        return pltpu.make_async_remote_copy(
            src_ref=src, dst_ref=dst, send_sem=ssem, recv_sem=rsem,
            device_id={"tile": dev}, device_id_type=MESH,
        )

    load_in = pltpu.make_async_copy(bin_hbm, bi, basis_sem.at[0])
    load_out = pltpu.make_async_copy(bout_hbm, bo, basis_sem.at[1])
    load_in.start()
    load_out.start()

    barrier = pltpu.get_barrier_semaphore()

    def greet(i, carry):
        pl.semaphore_signal(
            barrier, inc=1, device_id={"tile": lax.rem(me + i, n)}, device_id_type=MESH
        )
        return carry

    lax.fori_loop(1, n, greet, 0)
    pl.semaphore_wait(barrier, n - 1)

    def tok_copy(to, frm):
        return remote(
            x.at[:, pl.ds(pl.multiple_of(to * depth, depth), depth)],
            r.at[frm], tok_s.at[to], tok_r.at[frm], to,
        )

    def send_tok(i, carry):
        tok_copy(lax.rem(me + i, n), me).start()
        return carry

    lax.fori_loop(1, n, send_tok, 0)
    r[pl.ds(me, 1)] = x[:, pl.ds(pl.multiple_of(me * depth, depth), depth)][None]

    def recv_tok(i, carry):
        tok_copy(me, lax.rem(me + n - i, n)).wait_recv()
        return carry

    lax.fori_loop(1, n, recv_tok, 0)
    both = r[...].astype(F32)
    a = both[:, :tok].reshape(n * tok, depth).astype(BF16)
    g = both[:, tok:].reshape(n * tok, depth).astype(BF16)
    load_out.wait()
    load_in.wait()


    def core_a(yy, zz):
        return remote(
            ca_send.at[yy, zz], ca_recv.at[yy, zz], ca_s.at[yy, zz], ca_r.at[yy, zz], sib
        )

    def core_g(yy, zz):
        return remote(
            cg_send.at[yy, zz], cg_recv.at[yy, zz], cg_s.at[yy, zz], cg_r.at[yy, zz], sib
        )

    def acol(cc, yy, zz):
        start = ((cc * YS + yy) * zs + zz) * acols
        return pl.ds(pl.multiple_of(start, acols), acols)

    def send_a(yy, zz):
        ca_send[yy, zz] = jnp.dot(a, bi[:, acol(oc, yy, zz)], preferred_element_type=F32)
        core_a(yy, zz).start()

    def keep_a(yy, zz):
        ca_own[yy, zz] = jnp.dot(a, bi[:, acol(c, yy, zz)], preferred_element_type=F32)

    def make_g(yy, zz):
        gpart = jnp.dot(
            g,
            bo[:, pl.ds(pl.multiple_of((zz * YS + yy) * gcols, gcols), gcols)],
            preferred_element_type=F32,
        )
        low, high = gpart[:half_rows], gpart[half_rows:]
        cg_send[yy, zz] = jnp.where(c == 0, high, low)
        core_g(yy, zz).start()
        cg_own[yy, zz] = jnp.where(c == 0, low, high)

    def rows(h):
        return pl.ds(h * half_rows, half_rows)

    def y_a(h, zz):
        return remote(
            ya_send.at[zz, rows(h)], ya_recv.at[zz, rows(h)], ya_s.at[h, zz], ya_r.at[h, zz], yp
        )

    def y_g(zz):
        return remote(yg_send.at[zz], yg_recv.at[zz], yg_s.at[zz], yg_r.at[zz], yp)

    def zdev(zz):
        return zz * (CORES * YS) + lax.rem(me, CORES * YS)

    def z_a(h, to, frm):
        return remote(
            za_send.at[to, rows(h)], za_recv.at[frm, rows(h)],
            za_s.at[h, to], za_r.at[h, frm], zdev(to),
        )

    def z_g(to, frm):
        return remote(zg_send.at[to], zg_recv.at[frm], zg_s.at[to], zg_r.at[frm], zdev(to))

    order = [lax.rem(z + 1 + i, zs) for i in range(zs)]

    others = [lax.rem(z + zs - 1 - i, zs) for i in range(zs - 1)]

    for zz in order:
        send_a(oy, zz)
    for zz in order:
        keep_a(oy, zz)
        core_a(oy, zz).wait_recv()
        ya_send[zz] = (ca_own[oy, zz] + ca_recv[oy, zz]).astype(BF16)
        y_a(0, zz).start()
    for zz in order:
        y_a(1, zz).start()
    for zz in order:
        send_a(y, zz)
        keep_a(y, zz)
    for zz in order:
        make_g(oy, zz)

    def finish_a(h, i):
        zz = order[i]
        y_a(h, zz).wait_recv()
        at = rows(h)
        total = ca_own[y, zz, at] + ca_recv[y, zz, at] + ya_recv[zz, at].astype(F32)
        if i < zs - 1:
            za_send[zz, at] = total.astype(BF16)
            z_a(h, zz, z).start()
        else:
            ca_own[y, zz, at] = total

    for i, zz in enumerate(order):
        core_a(y, zz).wait_recv()
        finish_a(0, i)
        core_g(oy, zz).wait_recv()
        yg_send[zz] = (cg_own[oy, zz] + cg_recv[oy, zz]).astype(BF16)
    for i, zz in enumerate(order):
        finish_a(1, i)
        y_g(zz).start()
        make_g(y, zz)

    def ag_z(h, to, frm):
        block = ag.at[y, frm, rows(h)]
        return remote(block, block, agz_s.at[h, to], agz_r.at[h, frm], zdev(to))

    def ag_y(h, yy, zz):
        block = ag.at[yy, zz, rows(h)]
        return remote(block, block, agy_s.at[h, zz], agy_r.at[h, zz], yp)

    def gather_a(h):
        at = rows(h)
        total = ca_own[y, z, at]
        for zz in others:
            z_a(h, z, zz).wait_recv()
            total = total + za_recv[zz, at].astype(F32)
        ag[y, z, at] = total.astype(BF16)
        for zz in order[:-1]:
            ag_z(h, zz, z).start()
        ag_y(h, y, z).start()

    def forward_a(h):
        for zz in others:
            ag_z(h, z, zz).wait_recv()
            ag_y(h, y, zz).start()

    gather_a(0)
    gather_a(1)

    def finish_g(i):
        zz = order[i]
        core_g(y, zz).wait_recv()
        y_g(zz).wait_recv()
        total = cg_own[y, zz] + cg_recv[y, zz] + yg_recv[zz].astype(F32)
        if i < zs - 1:
            zg_send[zz] = total.astype(BF16)
            z_g(zz, z).start()
        else:
            cg_own[y, zz] = total

    finish_g(0)
    finish_g(1)
    forward_a(0)
    for i in range(2, zs):
        finish_g(i)
    forward_a(1)

    total = cg_own[y, z]
    for zz in others:
        z_g(z, zz).wait_recv()
        total = total + zg_recv[zz].astype(F32)
    gx[c] = total
    swap = remote(gx.at[c], gx.at[c], gx_s, gx_r, sib)
    swap.start()
    aout_ref[y] = ag[y]
    remote(gx.at[oc], gx.at[oc], gx_s, gx_r, sib).wait_recv()
    gt = gx[...].reshape(CORES * half_rows, gcols).T
    high = gt.astype(BF16)
    gout_ref[:, : CORES * half_rows] = high
    gout_ref[:, CORES * half_rows :] = (gt - high.astype(F32)).astype(BF16)
    for zz in [z] + others:
        ag_y(0, oy, zz).wait_recv()
        ag_y(1, oy, zz).wait_recv()
        aout_ref[oy, zz] = ag[oy, zz]

    def sent_tok(i, carry):
        tok_copy(lax.rem(me + i, n), me).wait_send()
        return carry

    lax.fori_loop(1, n, sent_tok, 0)
    for zz in order:
        core_a(oy, zz).wait_send()
        core_g(oy, zz).wait_send()
        core_a(y, zz).wait_send()
        core_g(y, zz).wait_send()
        y_a(0, zz).wait_send()
        y_a(1, zz).wait_send()
        y_g(zz).wait_send()
        ag_y(0, y, zz).wait_send()
        ag_y(1, y, zz).wait_send()
    for zz in order[:-1]:
        z_a(0, zz, z).wait_send()
        z_a(1, zz, z).wait_send()
        z_g(zz, z).wait_send()
        ag_z(0, zz, z).wait_send()
        ag_z(1, zz, z).wait_send()
    swap.wait_send()


def rotate(acts, grads, basis_in, basis_out, tiles):
    zs = tiles // (CORES * YS)
    tok, width_in = acts.shape
    width_out = grads.shape[1]
    depth = basis_in.shape[0]
    tokens = tok * tiles
    half = tokens // CORES
    acols = width_in // tiles
    gcols = width_out // ROWB
    a_grid, g_grid = (YS, zs, tokens, acols), (YS, zs, half, gcols)
    dma = pltpu.SemaphoreType.DMA
    scratch = [
        pltpu.VMEM((tiles, 2 * tok, depth), BF16),
        pltpu.VMEM((depth, width_in), BF16),
        pltpu.VMEM((depth, width_out), BF16),
    ]
    scratch += [pltpu.VMEM(a_grid, F32)] * 3 + [pltpu.VMEM(g_grid, F32)] * 3
    for _ in range(2):
        scratch += [pltpu.VMEM(a_grid[1:], BF16)] * 2 + [pltpu.VMEM(g_grid[1:], BF16)] * 2
    scratch += [pltpu.VMEM(a_grid, BF16), pltpu.VMEM((CORES, half, gcols), F32)]
    scratch += [dma((2,)), dma((tiles,)), dma((tiles,))]
    scratch += [dma((YS, zs))] * 4 + ([dma((2, zs))] * 2 + [dma((zs,))] * 2) * 2 + [dma((2, zs))] * 4 + [dma, dma]
    return pl.pallas_call(
        functools.partial(rotate_kernel, zs),
        out_shape=(
            jax.ShapeDtypeStruct(a_grid, BF16),
            jax.ShapeDtypeStruct((gcols, 2 * tokens), BF16),
        ),
        in_specs=[pl.BlockSpec(memory_space=pltpu.VMEM)]
        + [pl.BlockSpec(memory_space=pl.ANY)] * 2,
        out_specs=(pl.BlockSpec(memory_space=pltpu.VMEM),) * 2,
        scratch_shapes=scratch,
        compiler_params=pltpu.CompilerParams(
            collective_id=0, has_side_effects=True, vmem_limit_bytes=VMEM_LIMIT
        ),
        name="rotate",
    )(jnp.concatenate([acts, grads], axis=0), basis_in, basis_out)


def correct_kernel(scale, a_ref, g_ref, out_ref):
    acols = a_ref.shape[2]
    for k in range(a_ref.shape[0]):
        a = a_ref[k]
        rotated = jnp.dot(
            g_ref[...], jnp.concatenate([a, a], axis=0), preferred_element_type=F32
        )
        out_ref[0, :, k * acols : (k + 1) * acols] = rotated * rotated * scale


def correct(a, g):
    blocks, tokens, acols = a.shape
    rows = g.shape[0]
    step = 2
    return pl.pallas_call(
        functools.partial(correct_kernel, 1.0 / tokens),
        grid=(blocks // step,),
        out_shape=jax.ShapeDtypeStruct((1, rows, blocks * acols), F32),
        in_specs=[
            pl.BlockSpec((step, tokens, acols), lambda i: (i, 0, 0)),
            pl.BlockSpec((rows, 2 * tokens), lambda i: (0, 0)),
        ],
        out_specs=pl.BlockSpec((1, rows, step * acols), lambda i: (0, 0, i)),
        compiler_params=pltpu.CompilerParams(vmem_limit_bytes=16 * 1024 * 1024),
        name="correct",
    )(a, g)


def chip_body(acts, grads, basis_in, basis_out):
    tiles = lax.axis_size("tile")
    a, g = rotate(acts, grads, basis_in, basis_out, tiles)
    tokens = a.shape[2]
    return correct(a.reshape(-1, tokens, a.shape[3]), g)


def body(acts, grads, basis_in, basis_out):
    tiles = lax.axis_size("tile")
    tok_rows = acts.shape[0]
    width_in = acts.shape[1]
    width_out = grads.shape[1]
    col_blocks = tiles // ROWB
    tile_rows_n = width_out // ROWB
    tile_cols_n = width_in // col_blocks
    acts_feat, grads_feat = (
        lax.all_to_all(acts, "tile", split_axis=1, concat_axis=0, tiled=True),
        lax.all_to_all(grads, "tile", split_axis=1, concat_axis=0, tiled=True),
    )
    acts_rot = lax.psum_scatter(
        jnp.dot(acts_feat, basis_in, preferred_element_type=jnp.float32),
        "tile",
        scatter_dimension=0,
        tiled=True,
    ).astype(jnp.bfloat16)
    grads_rot = lax.psum_scatter(
        jnp.dot(grads_feat, basis_out, preferred_element_type=jnp.float32),
        "tile",
        scatter_dimension=0,
        tiled=True,
    ).astype(jnp.bfloat16)
    grad_send = jnp.repeat(grads_rot.reshape(tok_rows, ROWB, tile_rows_n), col_blocks, axis=1)
    act_send = jnp.tile(acts_rot.reshape(tok_rows, col_blocks, tile_cols_n), (1, ROWB, 1))
    grad_tile, act_tile = (
        lax.all_to_all(grad_send, "tile", split_axis=1, concat_axis=0, tiled=True),
        lax.all_to_all(act_send, "tile", split_axis=1, concat_axis=0, tiled=True),
    )
    grad_tile = grad_tile.reshape(tok_rows * tiles, tile_rows_n)
    act_tile = act_tile.reshape(tok_rows * tiles, tile_cols_n)
    total_rows = grad_tile.shape[0]
    examples = total_rows // SEQ
    grad_ex = grad_tile.reshape(examples, SEQ, tile_rows_n)
    act_ex = act_tile.reshape(examples, SEQ, tile_cols_n)

    def accumulate(index, total):
        grad_part = grad_ex[index]
        act_part = act_ex[index]
        rotated = lax.dot_general(
            grad_part, act_part, (((0,), (0,)), ((), ())), preferred_element_type=jnp.float32
        )
        return total + rotated * rotated

    start = jnp.zeros((tile_rows_n, tile_cols_n), jnp.float32)
    total = lax.fori_loop(0, examples, accumulate, start)
    corr = total / float(examples * SEQ)
    return corr[None]


def solution(mesh):
    in_specs = (
        P(("grp", "tile"), None),
        P(("grp", "tile"), None),
        P("tile", None),
        P("tile", None),
    )
    out_specs = P(("grp", "tile"), None, None)

    def whole(acts, grads, basis_in, basis_out):
        tiles = mesh.shape["tile"]
        tokens = acts.shape[0] // mesh.shape["grp"]
        per_chip = tiles == CORES * ROWB and tokens == SEQ
        return jax.shard_map(
            chip_body if per_chip else body,
            mesh=mesh, in_specs=in_specs, out_specs=out_specs, check_vma=False,
        )(acts, grads, basis_in, basis_out)

    return whole
```

```python
import functools

import jax
import jax.numpy as jnp
from jax import lax
from jax.experimental import pallas as pl
from jax.experimental.pallas import tpu as pltpu
from jax.sharding import PartitionSpec as P

SEQ = 128
ROWB = 8
CORES = 2
YS = 2
MESH = pl.DeviceIdType.MESH
VMEM_LIMIT = 52 * 1024 * 1024
F32 = jnp.float32
BF16 = jnp.bfloat16


def rotate_kernel(
    zs,
    x, bin_hbm, bout_hbm,
    aout_ref, gout_ref,
    r, bi, bo,
    ca_own, ca_send, ca_recv, cg_own, cg_send, cg_recv,
    ya_send, ya_recv, yg_send, yg_recv,
    za_send, za_recv, zg_send, zg_recv,
    ag, gx,
    basis_sem, tok_s, tok_r,
    ca_s, ca_r, cg_s, cg_r,
    ya_s, ya_r, yg_s, yg_r,
    za_s, za_r, zg_s, zg_r,
    agz_s, agz_r, agy_s, agy_r, gx_s, gx_r,
):
    n = CORES * YS * zs
    tok = x.shape[0] // 2
    depth = bi.shape[0]
    half_rows = gx.shape[1]
    gcols = gx.shape[2]
    acols = ag.shape[-1]
    me = lax.axis_index("tile")
    c = lax.rem(me, CORES)
    y = lax.rem(me // CORES, YS)
    z = me // (CORES * YS)
    sib = me + 1 - 2 * c
    yp = me + CORES * (1 - 2 * y)
    oc, oy = 1 - c, 1 - y

    def remote(src, dst, ssem, rsem, dev):
        return pltpu.make_async_remote_copy(
            src_ref=src, dst_ref=dst, send_sem=ssem, recv_sem=rsem,
            device_id={"tile": dev}, device_id_type=MESH,
        )

    load_in = pltpu.make_async_copy(bin_hbm, bi, basis_sem.at[0])
    load_out = pltpu.make_async_copy(bout_hbm, bo, basis_sem.at[1])
    load_in.start()
    load_out.start()

    barrier = pltpu.get_barrier_semaphore()

    def greet(i, carry):
        pl.semaphore_signal(
            barrier, inc=1, device_id={"tile": lax.rem(me + i, n)}, device_id_type=MESH
        )
        return carry

    lax.fori_loop(1, n, greet, 0)
    pl.semaphore_wait(barrier, n - 1)

    def tok_copy(to, frm):
        return remote(
            x.at[:, pl.ds(pl.multiple_of(to * depth, depth), depth)],
            r.at[frm], tok_s.at[to], tok_r.at[frm], to,
        )

    def send_tok(i, carry):
        tok_copy(lax.rem(me + i, n), me).start()
        return carry

    lax.fori_loop(1, n, send_tok, 0)
    r[pl.ds(me, 1)] = x[:, pl.ds(pl.multiple_of(me * depth, depth), depth)][None]

    def recv_tok(i, carry):
        tok_copy(me, lax.rem(me + n - i, n)).wait_recv()
        return carry

    lax.fori_loop(1, n, recv_tok, 0)
    both = r[...].astype(F32)
    a = both[:, :tok].reshape(n * tok, depth).astype(BF16)
    g = both[:, tok:].reshape(n * tok, depth).astype(BF16)
    load_out.wait()
    load_in.wait()


    def core_a(yy, zz):
        return remote(
            ca_send.at[yy, zz], ca_recv.at[yy, zz], ca_s.at[yy, zz], ca_r.at[yy, zz], sib
        )

    def core_g(yy, zz):
        return remote(
            cg_send.at[yy, zz], cg_recv.at[yy, zz], cg_s.at[yy, zz], cg_r.at[yy, zz], sib
        )

    def acol(cc, yy, zz):
        start = ((cc * YS + yy) * zs + zz) * acols
        return pl.ds(pl.multiple_of(start, acols), acols)

    def send_a(yy, zz):
        ca_send[yy, zz] = jnp.dot(a, bi[:, acol(oc, yy, zz)], preferred_element_type=F32)
        core_a(yy, zz).start()

    def keep_a(yy, zz):
        ca_own[yy, zz] = jnp.dot(a, bi[:, acol(c, yy, zz)], preferred_element_type=F32)

    def make_g(yy, zz):
        gpart = jnp.dot(
            g,
            bo[:, pl.ds(pl.multiple_of((zz * YS + yy) * gcols, gcols), gcols)],
            preferred_element_type=F32,
        )
        low, high = gpart[:half_rows], gpart[half_rows:]
        cg_send[yy, zz] = jnp.where(c == 0, high, low)
        core_g(yy, zz).start()
        cg_own[yy, zz] = jnp.where(c == 0, low, high)

    def rows(h):
        return pl.ds(h * half_rows, half_rows)

    def y_a(h, zz):
        return remote(
            ya_send.at[zz, rows(h)], ya_recv.at[zz, rows(h)], ya_s.at[h, zz], ya_r.at[h, zz], yp
        )

    def y_g(zz):
        return remote(yg_send.at[zz], yg_recv.at[zz], yg_s.at[zz], yg_r.at[zz], yp)

    def zdev(zz):
        return zz * (CORES * YS) + lax.rem(me, CORES * YS)

    def z_a(h, to, frm):
        return remote(
            za_send.at[to, rows(h)], za_recv.at[frm, rows(h)],
            za_s.at[h, to], za_r.at[h, frm], zdev(to),
        )

    def z_g(to, frm):
        return remote(zg_send.at[to], zg_recv.at[frm], zg_s.at[to], zg_r.at[frm], zdev(to))

    order = [lax.rem(z + 1 + i, zs) for i in range(zs)]

    others = [lax.rem(z + zs - 1 - i, zs) for i in range(zs - 1)]

    for zz in order:
        send_a(oy, zz)
    for zz in order:
        keep_a(oy, zz)
        core_a(oy, zz).wait_recv()
        ya_send[zz] = (ca_own[oy, zz] + ca_recv[oy, zz]).astype(BF16)
        y_a(0, zz).start()
    for zz in order:
        y_a(1, zz).start()
    for zz in order:
        send_a(y, zz)
        keep_a(y, zz)
    for zz in order:
        make_g(oy, zz)
    for zz in order:
        make_g(y, zz)

    def finish_a(h, i):
        zz = order[i]
        y_a(h, zz).wait_recv()
        at = rows(h)
        total = ca_own[y, zz, at] + ca_recv[y, zz, at] + ya_recv[zz, at].astype(F32)
        if i < zs - 1:
            za_send[zz, at] = total.astype(BF16)
            z_a(h, zz, z).start()
        else:
            ca_own[y, zz, at] = total

    for i, zz in enumerate(order):
        core_a(y, zz).wait_recv()
        finish_a(0, i)
        core_g(oy, zz).wait_recv()
        yg_send[zz] = (cg_own[oy, zz] + cg_recv[oy, zz]).astype(BF16)
    for i, zz in enumerate(order):
        finish_a(1, i)
        y_g(zz).start()

    def ag_z(h, to, frm):
        block = ag.at[y, frm, rows(h)]
        return remote(block, block, agz_s.at[h, to], agz_r.at[h, frm], zdev(to))

    def ag_y(h, yy, zz):
        block = ag.at[yy, zz, rows(h)]
        return remote(block, block, agy_s.at[h, zz], agy_r.at[h, zz], yp)

    def gather_a(h):
        at = rows(h)
        total = ca_own[y, z, at]
        for zz in others:
            z_a(h, z, zz).wait_recv()
            total = total + za_recv[zz, at].astype(F32)
        ag[y, z, at] = total.astype(BF16)
        for zz in order[:-1]:
            ag_z(h, zz, z).start()
        ag_y(h, y, z).start()

    def forward_a(h):
        for zz in others:
            ag_z(h, z, zz).wait_recv()
            ag_y(h, y, zz).start()

    gather_a(0)
    gather_a(1)

    def finish_g(i):
        zz = order[i]
        core_g(y, zz).wait_recv()
        y_g(zz).wait_recv()
        total = cg_own[y, zz] + cg_recv[y, zz] + yg_recv[zz].astype(F32)
        if i < zs - 1:
            zg_send[zz] = total.astype(BF16)
            z_g(zz, z).start()
        else:
            cg_own[y, zz] = total

    forward_a(0)
    finish_g(0)
    finish_g(1)
    for i in range(2, zs):
        finish_g(i)
    forward_a(1)

    total = cg_own[y, z]
    for zz in others:
        z_g(z, zz).wait_recv()
        total = total + zg_recv[zz].astype(F32)
    gx[c] = total
    swap = remote(gx.at[c], gx.at[c], gx_s, gx_r, sib)
    swap.start()
    aout_ref[y] = ag[y]
    remote(gx.at[oc], gx.at[oc], gx_s, gx_r, sib).wait_recv()
    gt = gx[...].reshape(CORES * half_rows, gcols).T
    high = gt.astype(BF16)
    gout_ref[:, : CORES * half_rows] = high
    gout_ref[:, CORES * half_rows :] = (gt - high.astype(F32)).astype(BF16)
    for zz in [z] + others:
        ag_y(0, oy, zz).wait_recv()
        ag_y(1, oy, zz).wait_recv()
        aout_ref[oy, zz] = ag[oy, zz]

    def sent_tok(i, carry):
        tok_copy(lax.rem(me + i, n), me).wait_send()
        return carry

    lax.fori_loop(1, n, sent_tok, 0)
    for zz in order:
        core_a(oy, zz).wait_send()
        core_g(oy, zz).wait_send()
        core_a(y, zz).wait_send()
        core_g(y, zz).wait_send()
        y_a(0, zz).wait_send()
        y_a(1, zz).wait_send()
        y_g(zz).wait_send()
        ag_y(0, y, zz).wait_send()
        ag_y(1, y, zz).wait_send()
    for zz in order[:-1]:
        z_a(0, zz, z).wait_send()
        z_a(1, zz, z).wait_send()
        z_g(zz, z).wait_send()
        ag_z(0, zz, z).wait_send()
        ag_z(1, zz, z).wait_send()
    swap.wait_send()


def rotate(acts, grads, basis_in, basis_out, tiles):
    zs = tiles // (CORES * YS)
    tok, width_in = acts.shape
    width_out = grads.shape[1]
    depth = basis_in.shape[0]
    tokens = tok * tiles
    half = tokens // CORES
    acols = width_in // tiles
    gcols = width_out // ROWB
    a_grid, g_grid = (YS, zs, tokens, acols), (YS, zs, half, gcols)
    dma = pltpu.SemaphoreType.DMA
    scratch = [
        pltpu.VMEM((tiles, 2 * tok, depth), BF16),
        pltpu.VMEM((depth, width_in), BF16),
        pltpu.VMEM((depth, width_out), BF16),
    ]
    scratch += [pltpu.VMEM(a_grid, F32)] * 3 + [pltpu.VMEM(g_grid, F32)] * 3
    for _ in range(2):
        scratch += [pltpu.VMEM(a_grid[1:], BF16)] * 2 + [pltpu.VMEM(g_grid[1:], BF16)] * 2
    scratch += [pltpu.VMEM(a_grid, BF16), pltpu.VMEM((CORES, half, gcols), F32)]
    scratch += [dma((2,)), dma((tiles,)), dma((tiles,))]
    scratch += [dma((YS, zs))] * 4 + ([dma((2, zs))] * 2 + [dma((zs,))] * 2) * 2 + [dma((2, zs))] * 4 + [dma, dma]
    return pl.pallas_call(
        functools.partial(rotate_kernel, zs),
        out_shape=(
            jax.ShapeDtypeStruct(a_grid, BF16),
            jax.ShapeDtypeStruct((gcols, 2 * tokens), BF16),
        ),
        in_specs=[pl.BlockSpec(memory_space=pltpu.VMEM)]
        + [pl.BlockSpec(memory_space=pl.ANY)] * 2,
        out_specs=(pl.BlockSpec(memory_space=pltpu.VMEM),) * 2,
        scratch_shapes=scratch,
        compiler_params=pltpu.CompilerParams(
            collective_id=0, has_side_effects=True, vmem_limit_bytes=VMEM_LIMIT
        ),
        name="rotate",
    )(jnp.concatenate([acts, grads], axis=0), basis_in, basis_out)


def correct_kernel(scale, a_ref, g_ref, out_ref):
    acols = a_ref.shape[2]
    for k in range(a_ref.shape[0]):
        a = a_ref[k]
        rotated = jnp.dot(
            g_ref[...], jnp.concatenate([a, a], axis=0), preferred_element_type=F32
        )
        out_ref[0, :, k * acols : (k + 1) * acols] = rotated * rotated * scale


def correct(a, g):
    blocks, tokens, acols = a.shape
    rows = g.shape[0]
    step = 4
    return pl.pallas_call(
        functools.partial(correct_kernel, 1.0 / tokens),
        grid=(blocks // step,),
        out_shape=jax.ShapeDtypeStruct((1, rows, blocks * acols), F32),
        in_specs=[
            pl.BlockSpec((step, tokens, acols), lambda i: (i, 0, 0)),
            pl.BlockSpec((rows, 2 * tokens), lambda i: (0, 0)),
        ],
        out_specs=pl.BlockSpec((1, rows, step * acols), lambda i: (0, 0, i)),
        compiler_params=pltpu.CompilerParams(vmem_limit_bytes=16 * 1024 * 1024),
        name="correct",
    )(a, g)


def chip_body(acts, grads, basis_in, basis_out):
    tiles = lax.axis_size("tile")
    a, g = rotate(acts, grads, basis_in, basis_out, tiles)
    tokens = a.shape[2]
    return correct(a.reshape(-1, tokens, a.shape[3]), g)


def body(acts, grads, basis_in, basis_out):
    tiles = lax.axis_size("tile")
    tok_rows = acts.shape[0]
    width_in = acts.shape[1]
    width_out = grads.shape[1]
    col_blocks = tiles // ROWB
    tile_rows_n = width_out // ROWB
    tile_cols_n = width_in // col_blocks
    acts_feat, grads_feat = (
        lax.all_to_all(acts, "tile", split_axis=1, concat_axis=0, tiled=True),
        lax.all_to_all(grads, "tile", split_axis=1, concat_axis=0, tiled=True),
    )
    acts_rot = lax.psum_scatter(
        jnp.dot(acts_feat, basis_in, preferred_element_type=jnp.float32),
        "tile",
        scatter_dimension=0,
        tiled=True,
    ).astype(jnp.bfloat16)
    grads_rot = lax.psum_scatter(
        jnp.dot(grads_feat, basis_out, preferred_element_type=jnp.float32),
        "tile",
        scatter_dimension=0,
        tiled=True,
    ).astype(jnp.bfloat16)
    grad_send = jnp.repeat(grads_rot.reshape(tok_rows, ROWB, tile_rows_n), col_blocks, axis=1)
    act_send = jnp.tile(acts_rot.reshape(tok_rows, col_blocks, tile_cols_n), (1, ROWB, 1))
    grad_tile, act_tile = (
        lax.all_to_all(grad_send, "tile", split_axis=1, concat_axis=0, tiled=True),
        lax.all_to_all(act_send, "tile", split_axis=1, concat_axis=0, tiled=True),
    )
    grad_tile = grad_tile.reshape(tok_rows * tiles, tile_rows_n)
    act_tile = act_tile.reshape(tok_rows * tiles, tile_cols_n)
    total_rows = grad_tile.shape[0]
    examples = total_rows // SEQ
    grad_ex = grad_tile.reshape(examples, SEQ, tile_rows_n)
    act_ex = act_tile.reshape(examples, SEQ, tile_cols_n)

    def accumulate(index, total):
        grad_part = grad_ex[index]
        act_part = act_ex[index]
        rotated = lax.dot_general(
            grad_part, act_part, (((0,), (0,)), ((), ())), preferred_element_type=jnp.float32
        )
        return total + rotated * rotated

    start = jnp.zeros((tile_rows_n, tile_cols_n), jnp.float32)
    total = lax.fori_loop(0, examples, accumulate, start)
    corr = total / float(examples * SEQ)
    return corr[None]


def solution(mesh):
    in_specs = (
        P(("grp", "tile"), None),
        P(("grp", "tile"), None),
        P("tile", None),
        P("tile", None),
    )
    out_specs = P(("grp", "tile"), None, None)

    def whole(acts, grads, basis_in, basis_out):
        tiles = mesh.shape["tile"]
        tokens = acts.shape[0] // mesh.shape["grp"]
        per_chip = tiles == CORES * ROWB and tokens == SEQ
        return jax.shard_map(
            chip_body if per_chip else body,
            mesh=mesh, in_specs=in_specs, out_specs=out_specs, check_vma=False,
        )(acts, grads, basis_in, basis_out)

    return whole
```
